32 devices in a mesh: row: 4 (over y, x), col: 8 (over z, core).
Axes of the slice: x: 2, y: 2, z: 4, core: 2. Of those that a mesh axis runs over, the one named last changes fastest.
Arguments:
- points: int32 [16, 3, 1024], P('row', None, 'col'), may hold values from 0 to 31
- ranks: int32 [16], replicated, may hold values from 64 to 256, as said below
- bases: bfloat16 [16, 1024, 256], P('row', 'col'), may hold values from -0.375 to 0.375
- pivots: bfloat16 [2, 256, 256], replicated, may hold values from -0.119628906 to 0.119628906
- probes: bfloat16 [16, 64, 1024], P('col'), may hold values from -0.119628906 to 0.119628906
Outputs:
- updated: bfloat16 [16, 16, 256, 256], P('row', 'col')
- images: float32 [16, 64, 1024], P('row', None, 'col')
The draws below stay inside these ranges and needn't reach their ends.
Inputs may be any that keep to these rules, and one draw needn't show every extreme that they name: `ranks`: the rank of each tile; some tile has rank 256 and some rank 256 // 4.
All inputs are finite; a program needn't handle non-finite values.
Results may differ from the reference program's by a relative error of at most 0.004.
The reference program's roundings to bfloat16 on the way count: a program that leaves them out, or rounds other values in their place, can miss the bound.
Values may be sent and summed in bfloat16 or wider, within the bound.
A program may use at most 64 MiB of HBM per device.

```python
import jax
import jax.numpy as jnp
from jax import lax

B = 1024
R = 256
PROBES = 64
PANELS = 2
GRID = 32
NT = 16


def draw_ranks(key, part):
    first, second, third = jax.random.split(jax.random.fold_in(key, 7), 3)
    values = jax.random.randint(first, (NT,), R // 4, R + 1)
    high_pos = jax.random.randint(second, (), 0, NT)
    low_pos = (high_pos + 1 + jax.random.randint(third, (), 0, NT - 1)) % NT
    values = values.at[high_pos].set(R)
    values = values.at[low_pos].set(R // 4)
    return values.astype(jnp.int32)


def place_ends(result, stream_key, smallest, top_value):
    place = [jax.random.randint(jax.random.fold_in(stream_key, axis), (), 0, length) for axis, length in enumerate(result.shape)]
    longest = result.shape.index(max(result.shape))
    next_to = place[:longest] + [(place[longest] + 1) % result.shape[longest]] + place[longest + 1:]
    return result.at[tuple(place)].set(smallest).at[tuple(next_to)].set(top_value)


def steps_of(key, dims, cuts, smallest, high):
    def one(dim, parts):
        heights = jax.random.uniform(jax.random.fold_in(jax.random.fold_in(key, 6), dim), (parts,), jnp.float32, smallest / len(cuts), high / len(cuts))
        return jnp.repeat(jnp.exp(heights), dims[dim] // parts).reshape((-1,) + (1,) * (len(dims) - dim - 1))

    gain = one(*cuts[0])
    for cut in cuts[1:]:
        gain = gain * one(*cut)
    return gain


def noise(key, extent, deviation, most, cuts=(), kind=jnp.bfloat16):
    values = deviation * jax.random.normal(key, extent, jnp.float32)
    if cuts:
        values = values * steps_of(key, extent, cuts, -0.22, 0.18)
    return jnp.clip(values, -most, most).astype(kind)


def setup_inputs(seed: int = 0) -> dict:
    key_list = jax.random.split(jax.random.key(seed), 6)
    points = place_ends(jax.random.randint(key_list[0], (NT, 3, B), 0, GRID), jax.random.fold_in(key_list[0], 1), 0, GRID - 1).astype(jnp.int32)
    ranks = draw_ranks(jax.random.fold_in(key_list[5], 71), 0)
    bases = noise(key_list[2], (NT, B, R), 0.0625, 0.375, ((0, 4), (1, 8)))
    pivots = noise(key_list[3], (PANELS, R, R), (0.32 / R ** 0.5), 0.119628906)
    probes = noise(key_list[4], (NT, PROBES, B), 0.02, 0.119628906, ((0, 8),))
    return dict(points=points, ranks=ranks, bases=bases, pivots=pivots, probes=probes)


nugget = 0.25
decay_length = 4.0
wave_length = 3.0

def kernel_tile(rows, cols):
    diff = rows[:, :, None] - cols[:, None, :]
    dist = jnp.sqrt(lax.optimization_barrier(jnp.sum(diff * diff, axis=0)) + nugget)
    return (jnp.exp(-dist / decay_length) * jnp.cos(dist / wave_length)).astype(jnp.bfloat16)

def reference(points, ranks, bases, pivots, probes):
    coords = points.astype(jnp.float32)
    rank_iota = jnp.arange(R, dtype=jnp.int32)
    masks = (rank_iota[None, :] < ranks[:, None]).astype(jnp.float32)
    tile_ids = jnp.arange(NT, dtype=jnp.int32)

    def row_cores(row_id):

        def one_core(col_id):
            tile = kernel_tile(coords[row_id], coords[col_id])
            proj = jnp.dot(tile, bases[col_id], preferred_element_type=jnp.float32).astype(jnp.bfloat16)
            core = jnp.dot(bases[row_id].T, proj, preferred_element_type=jnp.float32)
            return (core * masks[row_id][:, None] * masks[col_id][None, :]).astype(jnp.bfloat16)
        return lax.map(one_core, tile_ids)
    cores = lax.map(row_cores, tile_ids)
    left = jnp.einsum('ikab,kbc->ikac', cores[:, :PANELS].astype(jnp.float32), pivots.astype(jnp.float32)).astype(jnp.bfloat16)
    update = jnp.einsum('ikac,kjcd->ijad', left.astype(jnp.float32), cores[:PANELS].astype(jnp.float32))
    trailing = (tile_ids >= PANELS)[:, None] & (tile_ids >= PANELS)[None, :]
    updated = (cores.astype(jnp.float32) - jnp.where(trailing[:, :, None, None], update, 0.0)).astype(jnp.bfloat16)
    probe_cores = jnp.einsum('jpn,jnr->jpr', probes.astype(jnp.float32), bases.astype(jnp.float32)).astype(jnp.bfloat16)
    summed = jnp.einsum('ijab,jpb->ipa', updated.astype(jnp.float32), probe_cores.astype(jnp.float32))
    images = jnp.einsum('ipa,ina->ipn', summed, bases.astype(jnp.float32), precision=lax.Precision.HIGHEST)
    return (updated, images)
```

```python
import functools
import math

import jax
import jax.numpy as jnp
import numpy as np
from jax import lax
from jax.experimental import pallas as pl
from jax.experimental.pallas import tpu as pltpu
from jax.sharding import PartitionSpec as P

PANELS = 2
NUGGET = 0.25
DECAY = 4.0
WAVE = 3.0
FEATS = 16
BLK = 256
SPLIT = 32
LAG = 2
GROUPS = 2


def cosine_terms(count):
    k = np.arange(64)
    u = 0.125 * (1.0 + np.cos(np.pi * (k + 0.5) / 64))
    fit = np.polynomial.chebyshev.Chebyshev.fit(
        u, np.cos(2 * np.pi * np.sqrt(u)), count - 1, domain=[0.0, 0.25]
    )
    return [float(v) for v in fit.convert(kind=np.polynomial.Polynomial).coef]


COS = cosine_terms(7)


def mixer():
    m = np.zeros((FEATS, FEATS), np.float32)
    for a in range(3):
        m[a, a] = -2.0
    m[5, 3] = m[5, 4] = 1.0
    m[3, 5] = m[4, 6] = 1.0
    m[5, 6] = NUGGET
    return m


def covariance(s):
    dist = s * lax.rsqrt(s)
    turns = dist * (1.0 / (2.0 * math.pi * WAVE))
    g = turns - jnp.round(turns)
    u = g * g
    c = COS[-1] * u + COS[-2]
    for v in COS[-3::-1]:
        c = c * u + v
    return (jnp.exp(dist * (-1.0 / DECAY)) * c).astype(jnp.bfloat16)


def xor(a, b, bits):
    return sum(((a // (1 << k) + b // (1 << k)) % 2) * (1 << k) for k in range(bits))


def kernel(
    n_row, n_col, points, ranks, bases, pivots, probes, mix,
    updated, images,
    fslot, tfull, tcol, lhs, rowb, colb, kmat, cores, rowp, colp, probec, part, rsbuf, total,
    f_s, f_r, t_s, t_r, b_s, rel_s, b_r, cl_s, c_s, c_r, rp_s, rp_r, cp_s, cp_r, rs_s, rs_r, ag_s, ag_r,
):
    nt_row, chunk, rank = bases.shape
    nt_col = probes.shape[0]
    size = probes.shape[2]
    tiles = nt_row * nt_col
    bits = n_row.bit_length() - 1
    nz = n_col // 2
    r = lax.axis_index("row")
    c = lax.axis_index("col")
    core = c % 2
    z = c // 2
    sib = z * 2 + (1 - core)
    per = nt_row // nt_col
    root = c // per
    off = (c - root * per) * nt_col

    def ring_place(v):
        out = v
        for k in range(1, bits):
            out = xor(out, v // (1 << k), bits)
        return out

    def ring_owner(v):
        return xor(v, v // 2, bits)

    q = ring_place(r)
    after = ring_owner((q + 1) % n_row)
    before = ring_owner((q + n_row - 1) % n_row)
    d = (q + n_row - ring_place(root)) % n_row
    dx = xor(r, root, bits)
    f32 = jnp.float32

    def copy(src, dst, ss, rs, row=None, col=None):
        return pltpu.make_async_remote_copy(
            src_ref=src, dst_ref=dst, send_sem=ss, recv_sem=rs,
            device_id=(r if row is None else row, c if col is None else col),
            device_id_type=pl.DeviceIdType.MESH,
        )

    barrier = pltpu.get_barrier_semaphore()
    for k in range(1, n_col):
        pl.semaphore_signal(barrier, inc=1, device_id=(r, (c + k) % n_col), device_id_type=pl.DeviceIdType.MESH)
    for k in range(1, n_row):
        pl.semaphore_signal(barrier, inc=1, device_id=((r + k) % n_row, c), device_id_type=pl.DeviceIdType.MESH)
    pl.semaphore_wait(barrier, n_col + n_row - 2)

    place = lax.broadcasted_iota(jnp.int32, (FEATS, chunk), 0)
    for i in range(nt_row):
        p = points[i]
        norm = p[0:1] * p[0:1] + p[1:2] * p[1:2] + p[2:3] * p[2:3]
        low = norm & 31
        value = jnp.where((place == 5) | (place == 6), 1, 0)
        for row, v in enumerate((p[0:1], p[1:2], p[2:3], norm - low, low)):
            value = jnp.where(place == row, v, value)
        fslot[c, i] = value.astype(f32).astype(jnp.bfloat16)

    def feat_copy(k):
        return copy(fslot.at[c], fslot.at[c], f_s.at[k], f_r.at[c], col=(c + k) % n_col)

    for k in range(1, n_col):
        feat_copy(k).start()

    def mine(slot):
        return rowb.at[:, pl.ds(pl.multiple_of(slot * chunk, chunk), chunk), :]

    def base_copy(m):
        return copy(bases, mine(c), b_s.at[m], b_r.at[c], col=((z + m) % nz) * 2 + core)

    sib_copy = copy(bases, mine(c), b_s.at[0], b_r.at[c], col=sib)

    def relay_copy(m):
        slot = ((z + m) % nz) * 2 + core
        return copy(mine(slot), mine(slot), rel_s.at[m], b_r.at[slot], col=sib)

    for m in range(1, nz):
        base_copy(m).start()
    sib_copy.start()
    rowb[:, pl.ds(pl.multiple_of(c * chunk, chunk), chunk), :] = bases[...]

    for k in range(1, n_col):
        slot = (c + k) % n_col
        copy(fslot.at[slot], fslot.at[slot], f_s.at[k], f_r.at[slot], col=slot).wait_recv()
    for k in range(n_col):
        tfull[:, :, k * chunk:(k + 1) * chunk] = fslot[k]

    def tcol_copy(k):
        return copy(tcol, tcol, t_s.at[k], t_r, row=(r + k) % n_row)

    @pl.when(d == 0)
    def _():
        for j in range(nt_col):
            tcol[j] = tfull[off + j]
        for k in range(1, n_row):
            tcol_copy(k).start()

    for i in range(nt_row):
        lhs[i] = lax.dot_general(
            tfull[i], mix[...], (((0,), (0,)), ((), ())), preferred_element_type=f32
        ).astype(jnp.bfloat16)

    @pl.when(d != 0)
    def _():
        tcol_copy(1).wait_recv()

    nblk = size // BLK

    def k_step(n, _):
        t = n // nblk
        rows = pl.ds(pl.multiple_of((n % nblk) * BLK, BLK), BLK)
        s = jnp.dot(lhs[t // nt_col, rows, :], tcol[t % nt_col], preferred_element_type=f32)
        kmat[t, rows, :] = covariance(s)
        return 0

    def run(a, b):
        lax.fori_loop(a, b, k_step, 0)

    span = 2 * chunk

    def piece(m, j):
        rows = pl.ds(pl.multiple_of(((z + m) % nz) * span, span), span)
        return colb.at[j, rows, :], rows

    def piece_copy(m, j, b):
        ref, _ = piece(m, j)
        return copy(ref, ref, c_s.at[m, j, b], c_r.at[m, j], row=xor(r, 1 << b, bits))

    def has_child(j, b):
        if j % 2 == 0:
            return dx < (1 << b)
        return dx % (2 << b) == 0

    def forward(m, go):
        for j in range(nt_col):
            for b in range(bits):
                @pl.when(has_child(j, b))
                def _():
                    if go:
                        piece_copy(m, j, b).start()
                    else:
                        piece_copy(m, j, b).wait_send()

    def root_piece(m):
        @pl.when(dx == 0)
        def _():
            for j in range(nt_col):
                ref, rows = piece(m, j)
                local = pltpu.make_async_copy(rowb.at[off + j, rows, :], ref, cl_s.at[m, j])
                local.start()
                local.wait()
            forward(m, True)

    def other_piece(m):
        @pl.when(dx != 0)
        def _():
            for j in range(nt_col):
                piece_copy(m, j, 0).wait_recv()
            forward(m, True)

    def wait_slot(slot):
        copy(bases, mine(slot), b_s.at[0], b_r.at[slot], col=sib).wait_recv()

    marks = [SPLIT * (k + 1) // (nz + 1) for k in range(nz + 1)]
    done = 0
    for m in range(nz + 1):
        run(done, marks[m])
        done = marks[m]
        if m + 1 < nz:
            wait_slot(((z + m + 1) % nz) * 2 + core)
            relay_copy(m + 1).start()
        if m < nz:
            wait_slot(((z + m) % nz) * 2 + (1 - core))
            root_piece(m)
        if m >= 1:
            other_piece(m - 1)

    for j in range(nt_col):
        probec[j] = jnp.dot(probes[j], colb[j], preferred_element_type=f32).astype(jnp.bfloat16)

    def chain_copy(t, k=1):
        return copy(rowp.at[t], rowp.at[t], rp_s.at[k, t], rp_r.at[t], col=((z + k) % nz) * 2)

    def pair_copy(t):
        return copy(rowp.at[t], rowp.at[t], rp_s.at[0, t], rp_r.at[t], col=z * 2 + 1)

    def colp_copy(t, k=1):
        return copy(colp.at[t], colp.at[t], cp_s.at[k, t], cp_r.at[t], row=(r + k) % n_row)

    def pass_on(t):
        @pl.when(c != 0)
        def _():
            chain_copy(t).wait_recv()

        @pl.when(core == 0)
        def _():
            pair_copy(t).start()

            @pl.when(z == 0)
            def _():
                for k in range(1, nz):
                    chain_copy(t, k).start()

    def tile_step(t, _):
        i = t // nt_col
        j = t % nt_col
        extra = nblk * tiles - SPLIT
        lax.fori_loop(SPLIT + t * extra // tiles, SPLIT + (t + 1) * extra // tiles, k_step, 0)
        proj = jnp.dot(kmat[t], colb[j], preferred_element_type=f32).astype(jnp.bfloat16)
        raw = lax.dot_general(rowb[i], proj, (((0,), (0,)), ((), ())), preferred_element_type=f32)
        down = lax.broadcasted_iota(jnp.int32, (rank, rank), 0) < ranks[r * nt_row + i]
        across = lax.broadcasted_iota(jnp.int32, (rank, rank), 1) < ranks[c * nt_col + j]
        tile = jnp.where(down & across, raw, 0.0).astype(jnp.bfloat16)
        cores[t] = tile

        @pl.when(jnp.logical_and(r == 0, t < PANELS * nt_col))
        def _():
            colp[t] = tile
            for k in range(1, n_row):
                colp_copy(t, k).start()

        @pl.when(c == 0)
        def _():
            rowp[t] = tile
            pass_on(t)

        @pl.when(jnp.logical_and(c != 0, t >= LAG))
        def _():
            pass_on(t - LAG)

        return 0

    lax.fori_loop(0, tiles, tile_step, 0)

    @pl.when(r != 0)
    def _():
        for t in range(PANELS * nt_col):
            colp_copy(t).wait_recv()

    count = probes.shape[1]
    group = part.shape[0] // GROUPS
    height = group // n_col

    def cut(g, slot):
        return pl.ds(pl.multiple_of(g * group + slot * height, height), height)

    def rs_copy(g, k):
        slot = (c + k) % n_col
        return copy(part.at[cut(g, slot), :], rsbuf.at[g, c], rs_s.at[g, k], rs_r.at[g, c], col=slot)

    def ag_copy(g, k):
        rows = total.at[cut(g, c), :]
        return copy(rows, rows, ag_s.at[g, k], ag_r.at[g, c], col=(c + k) % n_col)

    def update_row(i):
        lefts = [
            jnp.dot(rowp[i * PANELS + k], pivots[k], preferred_element_type=f32).astype(jnp.bfloat16)
            for k in range(PANELS)
        ]
        acc = jnp.zeros((count, rank), f32)
        for j in range(nt_col):
            change = sum(
                jnp.dot(lefts[k], colp[k * nt_col + j], preferred_element_type=f32) for k in range(PANELS)
            )
            trailing = jnp.logical_and(r * nt_row + i >= PANELS, c * nt_col + j >= PANELS)
            new = cores[i * nt_col + j].astype(f32) - jnp.where(trailing, change, 0.0)
            new = new.astype(jnp.bfloat16)
            updated[i, j] = new
            acc += lax.dot_general(probec[j], new, (((1,), (1,)), ((), ())), preferred_element_type=f32)
        part[i * count:(i + 1) * count, :] = acc

    def add_up(g):
        for k in range(1, n_col):
            slot = (c + k) % n_col
            copy(part.at[cut(g, c), :], rsbuf.at[g, slot], rs_s.at[g, k], rs_r.at[g, slot], col=slot).wait_recv()
        acc = rsbuf[g, 0]
        for k in range(1, n_col):
            acc += rsbuf[g, k]
        total[cut(g, c), :] = acc
        for k in range(1, n_col):
            ag_copy(g, k).start()

    for i in range(nt_row):
        for t in range(max(tiles - LAG, i * PANELS), min(tiles, (i + 1) * PANELS)):
            @pl.when(c != 0)
            def _():
                pass_on(t)

        update_row(i)
        if (i + 1) * GROUPS % nt_row == 0:
            g = (i + 1) * GROUPS // nt_row - 1
            for k in range(1, n_col):
                rs_copy(g, k).start()
            rsbuf[g, c] = part[cut(g, c), :]
    for g in range(GROUPS):
        add_up(g)
    for g in range(GROUPS):
        for k in range(1, n_col):
            slot = (c + k) % n_col
            rows = total.at[cut(g, slot), :]
            copy(rows, rows, ag_s.at[g, k], ag_r.at[g, slot], col=slot).wait_recv()
    for i in range(nt_row):
        images[i] = lax.dot_general(
            total[i * count:(i + 1) * count, :], bases[i].astype(f32),
            (((1,), (1,)), ((), ())), precision=lax.Precision.HIGHEST, preferred_element_type=f32,
        )

    for k in range(1, n_col):
        feat_copy(k).wait_send()
        for g in range(GROUPS):
            rs_copy(g, k).wait_send()
            ag_copy(g, k).wait_send()

    @pl.when(d == 0)
    def _():
        for k in range(1, n_row):
            tcol_copy(k).wait_send()

    for m in range(1, nz):
        base_copy(m).wait_send()
        relay_copy(m).wait_send()
    sib_copy.wait_send()
    for m in range(nz):
        forward(m, False)

    @pl.when(r == 0)
    def _():
        for t in range(PANELS * nt_col):
            for k in range(1, n_row):
                colp_copy(t, k).wait_send()

    @pl.when(core == 0)
    def _():
        for t in range(tiles):
            pair_copy(t).wait_send()

        @pl.when(z == 0)
        def _():
            for t in range(tiles):
                for k in range(1, nz):
                    chain_copy(t, k).wait_send()


def body(n_row, n_col, points, ranks, bases, pivots, probes):
    nt_row, chunk, rank = bases.shape
    nt_col, count, size = probes.shape
    tiles = nt_row * nt_col
    bf = jnp.bfloat16
    f32 = jnp.float32
    nz = n_col // 2
    rows = nt_row * count
    dma = pltpu.SemaphoreType.DMA
    vmem = pl.BlockSpec(memory_space=pltpu.VMEM)
    flops = 2 * tiles * size * rank * (size + rank)
    return pl.pallas_call(
        functools.partial(kernel, n_row, n_col),
        out_shape=(
            jax.ShapeDtypeStruct((nt_row, nt_col, rank, rank), bf),
            jax.ShapeDtypeStruct((nt_row, count, chunk), f32),
        ),
        in_specs=[vmem, pl.BlockSpec(memory_space=pltpu.SMEM)] + [vmem] * 4,
        out_specs=(vmem, vmem),
        scratch_shapes=[
            pltpu.VMEM((n_col, nt_row, FEATS, chunk), bf),
            pltpu.VMEM((nt_row, FEATS, size), bf),
            pltpu.VMEM((nt_col, FEATS, size), bf),
            pltpu.VMEM((nt_row, size, FEATS), bf),
            pltpu.VMEM((nt_row, size, rank), bf),
            pltpu.VMEM((nt_col, size, rank), bf),
            pltpu.VMEM((tiles, size, size), bf),
            pltpu.VMEM((tiles, rank, rank), bf),
            pltpu.VMEM((nt_row * PANELS, rank, rank), bf),
            pltpu.VMEM((PANELS * nt_col, rank, rank), bf),
            pltpu.VMEM((nt_col, count, rank), bf),
            pltpu.VMEM((rows, rank), f32),
            pltpu.VMEM((GROUPS, n_col, rows // n_col // GROUPS, rank), f32),
            pltpu.VMEM((rows, rank), f32),
            dma((n_col,)), dma((n_col,)),
            dma((n_row,)), dma,
            dma((nz,)), dma((nz,)), dma((n_col,)),
            dma((nz, nt_col)), dma((nz, nt_col, n_row.bit_length() - 1)), dma((nz, nt_col)),
            dma((nz, tiles)), dma((tiles,)),
            dma((n_row, PANELS * nt_col)), dma((PANELS * nt_col,)),
            dma((GROUPS, n_col)), dma((GROUPS, n_col)), dma((GROUPS, n_col)), dma((GROUPS, n_col)),
        ],
        compiler_params=pltpu.CompilerParams(
            collective_id=0, has_side_effects=True, vmem_limit_bytes=56 * 1024 * 1024
        ),
        cost_estimate=pl.CostEstimate(
            flops=flops, bytes_accessed=4 << 20, transcendentals=2 * tiles * size * size
        ),
    )(points, ranks, bases, pivots, probes, jnp.asarray(mixer(), bf))


def solution(mesh):
    placed = (P("row", None, "col"), P(), P("row", "col", None), P(), P("col", None, None))
    return jax.shard_map(
        functools.partial(body, mesh.shape["row"], mesh.shape["col"]),
        mesh=mesh,
        in_specs=placed,
        out_specs=(P("row", "col", None, None), P("row", None, "col")),
        check_vma=False,
    )
```
